256 devices in a mesh: chan: 64 (over x, z_hi, y, core), slab: 4 (over z_lo).
Axes of the slice: x: 4, y: 4, z: 8 (z_hi: 2, z_lo: 4; z = z_hi * 4 + z_lo), core: 2. Of those that a mesh axis runs over, the one named last changes fastest.
Arguments:
- activations: bfloat16 [128, 8, 64, 128], P('chan', 'slab'), may hold values from -6 to 6
- cotangent: bfloat16 [128, 8, 64, 128], P('chan', 'slab'), may hold values from -6 to 6
- relu_mask: int32 [128, 8, 64, 128], P('chan', 'slab'), may hold values 0 or 1
- weights: bfloat16 [3, 3, 3, 128, 128], replicated, may hold values from -0.109375 to 0.109375
Outputs:
- pre: bfloat16 [128, 8, 64, 128], P('chan', 'slab')
- grad_input: bfloat16 [128, 8, 64, 128], P('chan', 'slab')
The draws below stay inside these ranges and needn't reach their ends.
All inputs are finite; a program needn't handle non-finite values. No bound on the sum of `relu_mask` on one device may be relied on, other than what follows from the above.
Results may differ from the reference program's by a relative error of at most 0.0013.
Values may be sent and summed in bfloat16 or wider, within the bound.
A program may use at most 64 MiB of HBM per device.

```python
import jax
import jax.numpy as jnp
from jax import lax

CHANNELS = 128
ROWS = 64
COLS = 128
DEPTH = 8


def place_ends(result, rng, smallest, top_value):
    place = [jax.random.randint(jax.random.fold_in(rng, axis), (), 0, length) for axis, length in enumerate(result.shape)]
    longest = result.shape.index(max(result.shape))
    beside = place[:longest] + [(place[longest] + 1) % result.shape[longest]] + place[longest + 1:]
    return result.at[tuple(place)].set(smallest).at[tuple(beside)].set(top_value)


def level_of(stream_key, dims, shards, low, largest):
    factor_of = 1.0
    for axis_at, blocks in shards:
        draws = jax.random.uniform(jax.random.fold_in(jax.random.fold_in(stream_key, 6), axis_at), (blocks,), jnp.float32, low / len(shards), largest / len(shards))
        factor_of = factor_of * jnp.repeat(jnp.exp(draws), dims[axis_at] // blocks).reshape((-1,) + (1,) * (len(dims) - 1 - axis_at))
    return factor_of


def bell_draw(rng, extent, deviation, limit, split=(), dtype=jnp.bfloat16):
    entries = jax.random.normal(rng, extent, jnp.float32) * deviation
    if len(split) > 0:
        entries = level_of(rng, extent, split, -0.22, 0.18) * entries
    return jnp.clip(entries, min=-limit, max=limit).astype(dtype)


def setup_inputs(seed: int = 0) -> dict:
    key_of = jax.random.split(jax.random.key(seed), 5)
    activations = bell_draw(key_of[0], (CHANNELS, DEPTH, ROWS, COLS), 1.0, 6.0, ((0, 64), (1, 4)))
    cotangent = bell_draw(key_of[1], (CHANNELS, DEPTH, ROWS, COLS), 1.0, 6.0, ((0, 64), (1, 4)))
    relu_mask = place_ends((jax.random.randint(key_of[2], (CHANNELS, DEPTH, ROWS, COLS), 0, 2) < 1).astype(jnp.int32), jax.random.fold_in(key_of[2], 1), 0, 1)
    weights = bell_draw(key_of[3], (3, 3, 3, CHANNELS, CHANNELS), (27 * CHANNELS) ** -0.5, 0.109375)
    return {"activations": activations, "cotangent": cotangent, "relu_mask": relu_mask, "weights": weights}


def convolve(inputs, kernel):
    return lax.conv_general_dilated(inputs, kernel, (1, 1, 1), ((1, 1), (1, 1), (1, 1)), dimension_numbers=('NCDHW', 'DHWOI', 'NCDHW'), precision=lax.Precision.HIGHEST)

def reference(activations, cotangent, relu_mask, weights):
    inputs = activations.astype(jnp.float32)[None]
    kernel = weights.astype(jnp.float32)
    pre = convolve(inputs, kernel)[0].astype(jnp.bfloat16)
    masked = jnp.where(relu_mask == 1, cotangent, jnp.zeros_like(cotangent))
    _, pullback = jax.vjp(lambda value: convolve(value, kernel), inputs)
    grad_input = pullback(masked.astype(jnp.float32)[None])[0][0].astype(jnp.bfloat16)
    return (pre, grad_input)
```

```python
import jax
import jax.numpy as jnp
from jax import lax
from jax.experimental import pallas as pl
from jax.experimental.pallas import tpu as pltpu
from jax.sharding import PartitionSpec as P

MESH = pl.DeviceIdType.MESH
BLOCKS = 32
LANES = 128


def spread(height):
    ch = lax.broadcasted_iota(jnp.int32, (3 * LANES, 1), 0)
    tap, ch = lax.shift_right_logical(ch, 7), lax.bitwise_and(ch, 127)
    at = lax.broadcasted_iota(jnp.int32, (1, 4 * LANES), 1)
    z_hi = lax.shift_right_logical(at, 8)
    source = lax.bitwise_and(lax.shift_right_logical(at, 3), 31)
    chan = lax.shift_right_logical(source, 3) * 16 + z_hi * 8 + lax.bitwise_and(source, 7)
    channel = 2 * chan + lax.bitwise_and(lax.shift_right_logical(at, 2), 1)
    hit = (ch == channel) & (lax.bitwise_and(at, 3) == tap + height)
    return jnp.where(hit, 1.0, 0.0).astype(jnp.bfloat16)


def kernel(act, cot, mask, weights, landed, act_v, cot_v, mask_v, w_v, padded, send, recv, taps, rows_f, units_f, out_send,
           in_sem, w_sem, send_sem, adj_sem, recv_sem, out_send_sem, out_recv_sem):
    chan, slab = lax.axis_index("chan"), lax.axis_index("slab")
    z_hi = (chan // 8) % 2
    core = chan % 2
    source = (chan // 16) * 8 + chan % 8
    worker = z_hi == 0
    pair = slab // 2
    work_pair = 1 - slab // 2
    work_adj = 2 - work_pair
    adj = (slab == 1) | (slab == 2)
    my_block = ((chan // 16) * 4 + (chan // 2) % 4) * 2 + slab % 2

    loads = [
        pltpu.make_async_copy(act, act_v, in_sem.at[0]),
        pltpu.make_async_copy(cot, cot_v, in_sem.at[1]),
        pltpu.make_async_copy(mask, mask_v, in_sem.at[2]),
    ]
    for load in loads:
        load.start()
    w_load = pltpu.make_async_copy(weights, w_v, w_sem)

    barrier = pltpu.get_barrier_semaphore()

    @pl.when(worker)
    def _():
        @pl.loop(0, 64)
        def _(other):
            for q in range(2):
                pl.semaphore_signal(barrier, inc=1, device_id=(other, 2 * work_pair + q), device_id_type=MESH)

            @pl.when((other != chan) | (work_adj != slab))
            def _():
                pl.semaphore_signal(barrier, inc=1, device_id=(other, work_adj), device_id_type=MESH)

        w_load.start()

    for load in loads:
        load.wait()
    for c in range(2):
        for ch in range(2):
            for p in range(2):
                padded[c, ch, p, 0:8, :] = jnp.zeros((8, LANES), jnp.float32)
                padded[c, ch, p, 72:80, :] = jnp.zeros((8, LANES), jnp.float32)
    for ch in range(2):
        for p in range(2):
            padded[0, ch, p, 8:72, :] = act_v[ch, p].astype(jnp.float32)
            padded[1, ch, p, 8:72, :] = jnp.where(mask_v[ch, p] == 1, cot_v[ch, p].astype(jnp.float32), 0.0)
    for b in range(BLOCKS):
        for c in range(2):
            for p in range(2):
                window = [padded[c, ch, p, 7 + 2 * b : 11 + 2 * b, :] for ch in range(2)]
                send[2 * b + c, p] = jnp.concatenate(window, axis=0).astype(jnp.bfloat16)

    itself = worker & adj
    pl.semaphore_wait(barrier, 64 + 64 * adj.astype(jnp.int32) - itself.astype(jnp.int32))

    def target(step, c, zb, of_pair):
        at = (step + chan // 2) % 16
        other = (at // 4) * 16 + (at % 4) * 2 + c
        return (other, 2 * (1 - of_pair) + zb), (at * 2 + zb) * 2 + c

    @pl.loop(0, 16)
    def _(step):
        for zb in range(2):
            for c in range(2):
                device, unit = target(step, c, zb, pair)
                pltpu.make_async_remote_copy(
                    src_ref=send.at[unit],
                    dst_ref=recv.at[z_hi, pl.ds(1 + 2 * (slab % 2), 2), source],
                    send_sem=send_sem,
                    recv_sem=recv_sem.at[z_hi],
                    device_id=device,
                    device_id_type=MESH,
                ).start()

    @pl.when(adj)
    def _():
        plane = 2 - slab
        there = 5 * (slab - 1)

        @pl.loop(0, 16)
        def _(step):
            for zb in range(2):
                for c in range(2):
                    (other, at_slab), unit = target(step, c, zb, 1 - pair)
                    remote = (other != chan) | (at_slab != slab)

                    @pl.when(remote)
                    def _():
                        pltpu.make_async_remote_copy(
                            src_ref=send.at[unit, plane],
                            dst_ref=recv.at[z_hi, there, source],
                            send_sem=adj_sem,
                            recv_sem=recv_sem.at[z_hi],
                            device_id=(other, at_slab),
                            device_id_type=MESH,
                        ).start()

                    @pl.when(jnp.logical_not(remote))
                    def _():
                        pltpu.make_async_copy(send.at[unit, plane], recv.at[z_hi, there, source], recv_sem.at[z_hi]).start()

    @pl.when(worker)
    def _():
        recv[:, 5 * work_pair] = jnp.zeros((2, 32, 8, LANES), jnp.bfloat16)
        w_load.wait()
        for height in range(2):
            places = spread(height)
            for i in range(3):

                @pl.loop(0, 3)
                def _(k):
                    at = pl.ds(pl.multiple_of(k * LANES, LANES), LANES)

                    @pl.when(core == 0)
                    def _():
                        left = jnp.concatenate([w_v[i, j, k] for j in range(3)], axis=1)
                        total = jnp.dot(left, places, preferred_element_type=jnp.float32)
                        taps[height, at, 512 * i : 512 * (i + 1)] = total.astype(jnp.bfloat16)

                    @pl.when(core == 1)
                    def _():
                        left = jnp.concatenate([w_v[2 - i, 2 - j, 2 - k] for j in range(3)], axis=0)
                        total = lax.dot_general(
                            left, places, (((0,), (0,)), ((), ())), preferred_element_type=jnp.float32
                        )
                        taps[height, at, 512 * i : 512 * (i + 1)] = total.astype(jnp.bfloat16)

        for half in range(2):
            here = recv.at[half, pl.ds(1 - work_pair, 5)]
            pltpu.make_async_copy(here, here, recv_sem.at[half]).wait()

        col = lax.broadcasted_iota(jnp.int32, (LANES, LANES), 1)
        for q in range(2):
            held = [
                [recv[half, 2 * q + i].reshape(256, LANES) for half in range(2)] for i in range(4)
            ]
            right = jnp.concatenate(
                [jnp.concatenate([held[i][half], held[i + 1][half]], axis=1) for i in range(3) for half in range(2)], axis=0
            )
            for height in range(2):
                part = jnp.dot(taps[height], right, preferred_element_type=jnp.float32)
                for p in range(2):
                    lanes = slice(LANES * p, LANES * (p + 1))
                    before, here, after = (part[LANES * k : LANES * (k + 1), lanes] for k in range(3))
                    total = (
                        here
                        + jnp.where(col == 0, 0.0, pltpu.roll(before, 1, 1))
                        + jnp.where(col == LANES - 1, 0.0, pltpu.roll(after, LANES - 1, 1))
                    )
                    rows_f[p, height] = total
            for p in range(2):
                for height in range(2):
                    for ch in range(2):
                        units_f[pl.ds(4 * p + 2 * height + ch, 64, stride=8), :] = rows_f[
                            p, height, pl.ds(ch, 64, stride=2), :
                        ]
            out_send[q] = units_f[...].astype(jnp.bfloat16).reshape(64, 8, LANES)

        for half in range(2):

            @pl.loop(0, 32)
            def _(step):
                other = (step // 8) * 16 + half * 8 + step % 8
                for q in range(2):
                    pltpu.make_async_remote_copy(
                        src_ref=out_send.at[q, other],
                        dst_ref=landed.at[core, my_block],
                        send_sem=out_send_sem,
                        recv_sem=out_recv_sem,
                        device_id=(other, 2 * work_pair + q),
                        device_id_type=MESH,
                    ).start()

    pltpu.make_async_copy(landed, landed, out_recv_sem).wait()

    pltpu.make_async_copy(send, send, send_sem).wait()

    @pl.when(adj & jnp.logical_not(worker))
    def _():
        half = send.at[pl.ds(0, 32)]
        pltpu.make_async_copy(half, half, adj_sem).wait()

    @pl.when(itself)
    def _():
        short = send.at[pl.ds(0, 63), 0]
        pltpu.make_async_copy(short, short, adj_sem).wait()

    @pl.when(worker)
    def _():
        pltpu.make_async_copy(out_send, out_send, out_send_sem).wait()


def order_rows(landed, pre, grad, landed_f, rows_f):
    for c, out in enumerate((pre, grad)):
        landed_f[...] = landed[c].reshape(BLOCKS * 8, LANES).astype(jnp.float32)
        for ch in range(2):
            for p in range(2):
                for height in range(2):
                    rows_f[pl.ds(height, BLOCKS, stride=2), :] = landed_f[
                        pl.ds(4 * p + 2 * height + ch, BLOCKS, stride=8), :
                    ]
                out[ch, p] = rows_f[...].astype(jnp.bfloat16)


def body(activations, cotangent, relu_mask, weights):
    bf16, f32 = jnp.bfloat16, jnp.float32
    vmem, anywhere = pl.BlockSpec(memory_space=pltpu.VMEM), pl.BlockSpec(memory_space=pl.ANY)
    dma = pltpu.SemaphoreType.DMA
    landed = pl.pallas_call(
        kernel,
        out_shape=jax.ShapeDtypeStruct((2, BLOCKS, 8, LANES), bf16),
        in_specs=[anywhere] * 4,
        out_specs=vmem,
        scratch_shapes=[
            pltpu.VMEM((2, 2, 64, LANES), bf16),
            pltpu.VMEM((2, 2, 64, LANES), bf16),
            pltpu.VMEM((2, 2, 64, LANES), jnp.int32),
            pltpu.VMEM((3, 3, 3, LANES, LANES), bf16),
            pltpu.VMEM((2, 2, 2, 80, LANES), f32),
            pltpu.VMEM((2 * BLOCKS, 2, 8, LANES), bf16),
            pltpu.VMEM((2, 6, 32, 8, LANES), bf16),
            pltpu.VMEM((2, 3 * LANES, 12 * LANES), bf16),
            pltpu.VMEM((2, 2, LANES, LANES), f32),
            pltpu.VMEM((64 * 8, LANES), f32),
            pltpu.VMEM((2, 64, 8, LANES), bf16),
            dma((3,)),
            dma,
            dma,
            dma,
            dma((2,)),
            dma,
            dma,
        ],
        compiler_params=pltpu.CompilerParams(
            collective_id=0, has_side_effects=True, vmem_limit_bytes=48 * 1024 * 1024
        ),
    )(activations, cotangent, relu_mask, weights)
    out = jax.ShapeDtypeStruct((2, 2, 64, LANES), bf16)
    return pl.pallas_call(
        order_rows,
        out_shape=(out, out),
        in_specs=[vmem],
        out_specs=(vmem, vmem),
        scratch_shapes=[pltpu.VMEM((BLOCKS * 8, LANES), f32), pltpu.VMEM((64, LANES), f32)],
    )(landed)


def solution(mesh):
    placed = (
        P("chan", "slab", None, None),
        P("chan", "slab", None, None),
        P("chan", "slab", None, None),
        P(),
    )
    return jax.shard_map(
        body,
        mesh=mesh,
        in_specs=placed,
        out_specs=(P("chan", "slab", None, None), P("chan", "slab", None, None)),
        check_vma=False,
    )
```

```python
import jax
import jax.numpy as jnp
from jax import lax
from jax.experimental import pallas as pl
from jax.experimental.pallas import tpu as pltpu
from jax.sharding import PartitionSpec as P

MESH = pl.DeviceIdType.MESH
BLOCKS = 32
LANES = 128


def spread(height):
    ch = lax.broadcasted_iota(jnp.int32, (3 * LANES, 1), 0)
    tap, ch = lax.shift_right_logical(ch, 7), lax.bitwise_and(ch, 127)
    at = lax.broadcasted_iota(jnp.int32, (1, 4 * LANES), 1)
    z_hi = lax.shift_right_logical(at, 8)
    source = lax.bitwise_and(lax.shift_right_logical(at, 3), 31)
    chan = lax.shift_right_logical(source, 3) * 16 + z_hi * 8 + lax.bitwise_and(source, 7)
    channel = 2 * chan + lax.bitwise_and(lax.shift_right_logical(at, 2), 1)
    hit = (ch == channel) & (lax.bitwise_and(at, 3) == tap + height)
    return jnp.where(hit, 1.0, 0.0).astype(jnp.bfloat16)


def kernel(act, cot, mask, weights, landed, act_v, cot_v, mask_v, w_v, padded, send, recv, taps, part_f, rows_f, units_f,
           out_send, in_sem, w_sem, send_sem, adj_sem, recv_sem, side_send_sem, side_recv_sem, out_send_sem,
           out_recv_sem):
    chan, slab = lax.axis_index("chan"), lax.axis_index("slab")
    z_hi = (chan // 8) % 2
    core = chan % 2
    beside = chan + 1 - 2 * core
    source = (chan // 16) * 8 + chan % 8
    pair = slab // 2
    adj = (slab == 1) | (slab == 2)
    my_block = ((chan // 16) * 4 + (chan // 2) % 4) * 2 + slab % 2
    work = 2 * (1 - slab // 2) + core
    work_inner = (work == 1) | (work == 2)
    work_adj = 3 - work
    itself = adj & (core == slab - 1)

    loads = [
        pltpu.make_async_copy(act, act_v, in_sem.at[0]),
        pltpu.make_async_copy(cot, cot_v, in_sem.at[1]),
        pltpu.make_async_copy(mask, mask_v, in_sem.at[2]),
    ]
    for load in loads:
        load.start()
    w_load = pltpu.make_async_copy(weights, w_v, w_sem)
    w_load.start()

    barrier = pltpu.get_barrier_semaphore()
    pl.semaphore_signal(barrier, inc=1, device_id=(beside, slab), device_id_type=MESH)
    for other in range(64):
        pl.semaphore_signal(barrier, inc=1, device_id=(other, work), device_id_type=MESH)

    @pl.when(work_inner)
    def _():
        @pl.loop(0, 64)
        def _(other):
            @pl.when((other != chan) | (work_adj != slab))
            def _():
                pl.semaphore_signal(barrier, inc=1, device_id=(other, work_adj), device_id_type=MESH)

    for load in loads:
        load.wait()
    for c in range(2):
        for ch in range(2):
            for p in range(2):
                padded[c, ch, p, 0:8, :] = jnp.zeros((8, LANES), jnp.float32)
                padded[c, ch, p, 72:80, :] = jnp.zeros((8, LANES), jnp.float32)
    for ch in range(2):
        for p in range(2):
            padded[0, ch, p, 8:72, :] = act_v[ch, p].astype(jnp.float32)
            padded[1, ch, p, 8:72, :] = jnp.where(mask_v[ch, p] == 1, cot_v[ch, p].astype(jnp.float32), 0.0)
    for b in range(BLOCKS):
        for c in range(2):
            for p in range(2):
                window = [padded[c, ch, p, 7 + 2 * b : 11 + 2 * b, :] for ch in range(2)]
                send[2 * b + c, p] = jnp.concatenate(window, axis=0).astype(jnp.bfloat16)

    pl.semaphore_wait(barrier, 65 + 64 * adj.astype(jnp.int32) - itself.astype(jnp.int32))

    for c in (1, 0):
        for b in range(BLOCKS):
            pltpu.make_async_remote_copy(
                src_ref=send.at[2 * b + c],
                dst_ref=recv.at[z_hi, pl.ds(1, 2), source],
                send_sem=send_sem,
                recv_sem=recv_sem.at[z_hi],
                device_id=((b // 8) * 16 + 8 * c + (b // 2 % 4) * 2 + slab % 2, 2 * (1 - pair) + b % 2),
                device_id_type=MESH,
            ).start()

    @pl.when(adj)
    def _():
        plane = 2 - slab
        there = 3 * (slab - 1)
        for c in (1, 0):

            @pl.loop(0, BLOCKS)
            def _(b):
                other, at_slab = (b // 8) * 16 + 8 * c + (b // 2 % 4) * 2 + slab - 1, 2 * pair + b % 2
                remote = (other != chan) | (at_slab != slab)

                @pl.when(remote)
                def _():
                    pltpu.make_async_remote_copy(
                        src_ref=send.at[2 * b + c, plane],
                        dst_ref=recv.at[z_hi, there, source],
                        send_sem=adj_sem,
                        recv_sem=recv_sem.at[z_hi],
                        device_id=(other, at_slab),
                        device_id_type=MESH,
                    ).start()

                @pl.when(jnp.logical_not(remote))
                def _():
                    pltpu.make_async_copy(send.at[2 * b + c, plane], recv.at[z_hi, there, source], recv_sem.at[z_hi]).start()

    @pl.when(jnp.logical_not(work_inner))
    def _():
        recv[:, work] = jnp.zeros((2, 32, 8, LANES), jnp.bfloat16)

    w_load.wait()
    for height in range(2):
        places = spread(height)
        for i in range(3):

            @pl.loop(0, 3)
            def _(k):
                at = pl.ds(pl.multiple_of(k * LANES, LANES), LANES)

                @pl.when(z_hi == 0)
                def _():
                    left = jnp.concatenate([w_v[i, j, k] for j in range(3)], axis=1)
                    total = jnp.dot(left, places, preferred_element_type=jnp.float32)
                    taps[i, height, at, :] = total.astype(jnp.bfloat16)

                @pl.when(z_hi == 1)
                def _():
                    left = jnp.concatenate([w_v[2 - i, 2 - j, 2 - k] for j in range(3)], axis=0)
                    total = lax.dot_general(
                        left, places, (((0,), (0,)), ((), ())), preferred_element_type=jnp.float32
                    )
                    taps[i, height, at, :] = total.astype(jnp.bfloat16)

    for half in range(2):

        @pl.when(work_inner)
        def _():
            here = recv.at[half, pl.ds(2 - work, 3)]
            pltpu.make_async_copy(here, here, recv_sem.at[half]).wait()

        @pl.when(jnp.logical_not(work_inner))
        def _():
            here = recv.at[half, pl.ds(1, 2)]
            pltpu.make_async_copy(here, here, recv_sem.at[half]).wait()

    side = pltpu.make_async_remote_copy(
        src_ref=recv.at[:, 2 - core],
        dst_ref=recv.at[:, 3 * core],
        send_sem=side_send_sem,
        recv_sem=side_recv_sem,
        device_id=(beside, slab),
        device_id_type=MESH,
    )
    side.start()

    def right(i):
        held = [[recv[half, i + p].reshape(256, LANES) for p in range(2)] for half in range(2)]
        return jnp.concatenate([jnp.concatenate(planes, axis=1) for planes in held], axis=0)

    last = 2 - 2 * core
    for height in range(2):
        part_f[height] = jnp.dot(
            taps[1, height], right(1), preferred_element_type=jnp.float32
        ) + jnp.dot(taps[2 - last, height], right(2 - last), preferred_element_type=jnp.float32)
    side.wait_recv()
    col = lax.broadcasted_iota(jnp.int32, (LANES, LANES), 1)
    for height in range(2):
        part = part_f[height] + jnp.dot(taps[last, height], right(last), preferred_element_type=jnp.float32)
        for p in range(2):
            lanes = slice(LANES * p, LANES * (p + 1))
            before, here, after = (part[LANES * k : LANES * (k + 1), lanes] for k in range(3))
            rows_f[p, height] = (
                here
                + jnp.where(col == 0, 0.0, pltpu.roll(before, 1, 1))
                + jnp.where(col == LANES - 1, 0.0, pltpu.roll(after, LANES - 1, 1))
            )
    for p in range(2):
        for height in range(2):
            for ch in range(2):
                units_f[pl.ds(4 * p + 2 * height + ch, 64, stride=8), :] = rows_f[p, height, pl.ds(ch, 64, stride=2), :]
    out_send[...] = units_f[...].astype(jnp.bfloat16).reshape(64, 8, LANES)

    for half in range(2):
        for step in range(32):
            other = (step // 8) * 16 + half * 8 + step % 8
            pltpu.make_async_remote_copy(
                src_ref=out_send.at[other],
                dst_ref=landed.at[z_hi, my_block],
                send_sem=out_send_sem,
                recv_sem=out_recv_sem,
                device_id=(other, work),
                device_id_type=MESH,
            ).start()

    pltpu.make_async_copy(landed, landed, out_recv_sem).wait()
    side.wait_send()
    pltpu.make_async_copy(send, send, send_sem).wait()

    @pl.when(adj & jnp.logical_not(itself))
    def _():
        sent = send.at[:, 0]
        pltpu.make_async_copy(sent, sent, adj_sem).wait()

    @pl.when(itself)
    def _():
        sent = send.at[pl.ds(0, 63), 0]
        pltpu.make_async_copy(sent, sent, adj_sem).wait()

    pltpu.make_async_copy(out_send, out_send, out_send_sem).wait()


def order_rows(landed, pre, grad, landed_f, rows_f):
    for c, out in enumerate((pre, grad)):
        landed_f[...] = landed[c].reshape(BLOCKS * 8, LANES).astype(jnp.float32)
        for ch in range(2):
            for p in range(2):
                for height in range(2):
                    rows_f[pl.ds(height, BLOCKS, stride=2), :] = landed_f[
                        pl.ds(4 * p + 2 * height + ch, BLOCKS, stride=8), :
                    ]
                out[ch, p] = rows_f[...].astype(jnp.bfloat16)


def body(activations, cotangent, relu_mask, weights):
    bf16, f32 = jnp.bfloat16, jnp.float32
    vmem, anywhere = pl.BlockSpec(memory_space=pltpu.VMEM), pl.BlockSpec(memory_space=pl.ANY)
    dma = pltpu.SemaphoreType.DMA
    landed = pl.pallas_call(
        kernel,
        out_shape=jax.ShapeDtypeStruct((2, BLOCKS, 8, LANES), bf16),
        in_specs=[anywhere] * 4,
        out_specs=vmem,
        scratch_shapes=[
            pltpu.VMEM((2, 2, 64, LANES), bf16),
            pltpu.VMEM((2, 2, 64, LANES), bf16),
            pltpu.VMEM((2, 2, 64, LANES), jnp.int32),
            pltpu.VMEM((3, 3, 3, LANES, LANES), bf16),
            pltpu.VMEM((2, 2, 2, 80, LANES), f32),
            pltpu.VMEM((2 * BLOCKS, 2, 8, LANES), bf16),
            pltpu.VMEM((2, 4, 32, 8, LANES), bf16),
            pltpu.VMEM((3, 2, 3 * LANES, 4 * LANES), bf16),
            pltpu.VMEM((2, 3 * LANES, 2 * LANES), f32),
            pltpu.VMEM((2, 2, LANES, LANES), f32),
            pltpu.VMEM((64 * 8, LANES), f32),
            pltpu.VMEM((64, 8, LANES), bf16),
            dma((3,)),
            dma,
            dma,
            dma,
            dma((2,)),
            dma,
            dma,
            dma,
            dma,
        ],
        compiler_params=pltpu.CompilerParams(
            collective_id=0, has_side_effects=True, vmem_limit_bytes=63 * 1024 * 1024
        ),
    )(activations, cotangent, relu_mask, weights)
    out = jax.ShapeDtypeStruct((2, 2, 64, LANES), bf16)
    return pl.pallas_call(
        order_rows,
        out_shape=(out, out),
        in_specs=[vmem],
        out_specs=(vmem, vmem),
        scratch_shapes=[pltpu.VMEM((BLOCKS * 8, LANES), f32), pltpu.VMEM((64, LANES), f32)],
    )(landed)


def solution(mesh):
    placed = (
        P("chan", "slab", None, None),
        P("chan", "slab", None, None),
        P("chan", "slab", None, None),
        P(),
    )
    return jax.shard_map(
        body,
        mesh=mesh,
        in_specs=placed,
        out_specs=(P("chan", "slab", None, None), P("chan", "slab", None, None)),
        check_vma=False,
    )
```

```python
import jax
import jax.numpy as jnp
from jax import lax
from jax.experimental import pallas as pl
from jax.experimental.pallas import tpu as pltpu
from jax.sharding import PartitionSpec as P

MESH = pl.DeviceIdType.MESH
BLOCKS = 32
LANES = 128


def spread(height):
    ch = lax.broadcasted_iota(jnp.int32, (3 * LANES, 1), 0)
    tap, ch = lax.shift_right_logical(ch, 7), lax.bitwise_and(ch, 127)
    at = lax.broadcasted_iota(jnp.int32, (1, 4 * LANES), 1)
    z_hi = lax.shift_right_logical(at, 8)
    source = lax.bitwise_and(lax.shift_right_logical(at, 3), 31)
    chan = lax.shift_right_logical(source, 3) * 16 + z_hi * 8 + lax.bitwise_and(source, 7)
    channel = 2 * chan + lax.bitwise_and(lax.shift_right_logical(at, 2), 1)
    hit = (ch == channel) & (lax.bitwise_and(at, 3) == tap + height)
    return jnp.where(hit, 1.0, 0.0).astype(jnp.bfloat16)


def kernel(act, cot, mask, weights, landed, act_v, cot_v, mask_v, w_v, padded, send, recv, taps, part_f, rows_f, units_f,
           out_send, in_sem, w_sem, send_sem, adj_sem, recv_sem, adj_recv_sem, side_send_sem, side_recv_sem, out_send_sem,
           out_recv_sem):
    chan, slab = lax.axis_index("chan"), lax.axis_index("slab")
    z_hi = (chan // 8) % 2
    core = chan % 2
    beside = chan + 1 - 2 * core
    source = (chan // 16) * 8 + chan % 8
    pair = slab // 2
    adj = (slab == 1) | (slab == 2)
    my_block = ((chan // 16) * 4 + (chan // 2) % 4) * 2 + slab % 2
    work = 2 * (1 - slab // 2) + core
    work_inner = (work == 1) | (work == 2)
    work_adj = 3 - work
    itself = adj & (core == slab - 1)

    loads = [
        pltpu.make_async_copy(act, act_v, in_sem.at[0]),
        pltpu.make_async_copy(cot, cot_v, in_sem.at[1]),
        pltpu.make_async_copy(mask, mask_v, in_sem.at[2]),
    ]
    for load in loads:
        load.start()
    w_load = pltpu.make_async_copy(weights, w_v, w_sem)
    w_load.start()

    barrier = pltpu.get_barrier_semaphore()
    pl.semaphore_signal(barrier, inc=1, device_id=(beside, slab), device_id_type=MESH)
    for other in range(64):
        pl.semaphore_signal(barrier, inc=1, device_id=(other, work), device_id_type=MESH)

    @pl.when(work_inner)
    def _():
        @pl.loop(0, 64)
        def _(other):
            @pl.when((other != chan) | (work_adj != slab))
            def _():
                pl.semaphore_signal(barrier, inc=1, device_id=(other, work_adj), device_id_type=MESH)

    for load in loads:
        load.wait()
    for c in range(2):
        for ch in range(2):
            for p in range(2):
                padded[c, ch, p, 0:8, :] = jnp.zeros((8, LANES), jnp.float32)
                padded[c, ch, p, 72:80, :] = jnp.zeros((8, LANES), jnp.float32)
    for ch in range(2):
        for p in range(2):
            padded[0, ch, p, 8:72, :] = act_v[ch, p].astype(jnp.float32)
            padded[1, ch, p, 8:72, :] = jnp.where(mask_v[ch, p] == 1, cot_v[ch, p].astype(jnp.float32), 0.0)
    for b in range(BLOCKS):
        for c in range(2):
            for p in range(2):
                window = [padded[c, ch, p, 7 + 2 * b : 11 + 2 * b, :] for ch in range(2)]
                send[2 * b + c, p] = jnp.concatenate(window, axis=0).astype(jnp.bfloat16)

    def make_taps(transposed):
        w_load.wait()
        for height in range(2):
            places = spread(height)
            for i in range(3):

                @pl.loop(0, 3)
                def _(k):
                    if transposed:
                        left = jnp.concatenate([w_v[2 - i, 2 - j, 2 - k] for j in range(3)], axis=0)
                        total = lax.dot_general(
                            left, places, (((0,), (0,)), ((), ())), preferred_element_type=jnp.float32
                        )
                    else:
                        left = jnp.concatenate([w_v[i, j, k] for j in range(3)], axis=1)
                        total = jnp.dot(left, places, preferred_element_type=jnp.float32)
                    at = pl.ds(pl.multiple_of(k * LANES, LANES), LANES)
                    for half in range(2):
                        taps[i, height, half, at, :] = total[:, 256 * half : 256 * (half + 1)].astype(jnp.bfloat16)

    @pl.when(z_hi == 0)
    def _():
        make_taps(False)

    pl.semaphore_wait(barrier, 65 + 64 * adj.astype(jnp.int32) - itself.astype(jnp.int32))

    for c in (1, 0):
        for b in range(BLOCKS):
            pltpu.make_async_remote_copy(
                src_ref=send.at[2 * b + c],
                dst_ref=recv.at[z_hi, pl.ds(1, 2), source],
                send_sem=send_sem,
                recv_sem=recv_sem.at[z_hi],
                device_id=((b // 8) * 16 + 8 * c + (b // 2 % 4) * 2 + slab % 2, 2 * (1 - pair) + b % 2),
                device_id_type=MESH,
            ).start()

    @pl.when(adj)
    def _():
        plane = 2 - slab
        there = 3 * (slab - 1)
        for c in (1, 0):
            for b in range(BLOCKS):
                other, at_slab = (b // 8) * 16 + 8 * c + (b // 2 % 4) * 2 + slab - 1, 2 * pair + b % 2

                @pl.when((other != chan) | (at_slab != slab))
                def _():
                    pltpu.make_async_remote_copy(
                        src_ref=send.at[2 * b + c, plane],
                        dst_ref=recv.at[z_hi, there, source],
                        send_sem=adj_sem,
                        recv_sem=adj_recv_sem.at[z_hi],
                        device_id=(other, at_slab),
                        device_id_type=MESH,
                    ).start()

        @pl.when(itself)
        def _():
            mine = send.at[2 * my_block + z_hi, plane]
            pltpu.make_async_copy(mine, recv.at[z_hi, there, source], adj_recv_sem.at[z_hi]).start()

    @pl.when(jnp.logical_not(work_inner))
    def _():
        recv[:, work] = jnp.zeros((2, 32, 8, LANES), jnp.bfloat16)

    @pl.when(z_hi == 1)
    def _():
        make_taps(True)

    def side(half):
        return pltpu.make_async_remote_copy(
            src_ref=recv.at[half, 2 - core],
            dst_ref=recv.at[half, 3 * core],
            send_sem=side_send_sem.at[half],
            recv_sem=side_recv_sem.at[half],
            device_id=(beside, slab),
            device_id_type=MESH,
        )

    def product(i, half, height):
        right = jnp.concatenate([recv[half, i + p].reshape(256, LANES) for p in range(2)], axis=1)
        return jnp.dot(taps[i, height, half], right, preferred_element_type=jnp.float32)

    last = 2 - 2 * core
    for turn in range(2):
        half = z_hi if turn == 0 else 1 - z_hi
        here = recv.at[half, pl.ds(1, 2)]
        pltpu.make_async_copy(here, here, recv_sem.at[half]).wait()
        side(half).start()
        for height in range(2):
            if turn == 0:
                part_f[height] = product(1, half, height)
            else:
                part_f[height] += product(1, half, height)

        @pl.when(work_inner)
        def _():
            here = recv.at[half, 3 * core]
            pltpu.make_async_copy(here, here, adj_recv_sem.at[half]).wait()

        for height in range(2):
            part_f[height] += product(2 - last, half, height)
        side(half).wait_recv()
        if turn == 0:
            for height in range(2):
                part_f[height] += product(last, half, height)

    col = lax.broadcasted_iota(jnp.int32, (LANES, LANES), 1)
    for height in range(2):
        part = part_f[height] + product(last, 1 - z_hi, height)
        for p in range(2):
            lanes = slice(LANES * p, LANES * (p + 1))
            before, here, after = (part[LANES * k : LANES * (k + 1), lanes] for k in range(3))
            rows_f[p, height] = (
                here
                + jnp.where(col == 0, 0.0, pltpu.roll(before, 1, 1))
                + jnp.where(col == LANES - 1, 0.0, pltpu.roll(after, LANES - 1, 1))
            )
    for p in range(2):
        for height in range(2):
            for ch in range(2):
                units_f[pl.ds(4 * p + 2 * height + ch, 64, stride=8), :] = rows_f[p, height, pl.ds(ch, 64, stride=2), :]
    out_send[...] = units_f[...].astype(jnp.bfloat16).reshape(64, 8, LANES)

    for half in range(2):
        for step in range(32):
            other = (step // 8) * 16 + half * 8 + step % 8
            pltpu.make_async_remote_copy(
                src_ref=out_send.at[other],
                dst_ref=landed.at[z_hi, my_block],
                send_sem=out_send_sem,
                recv_sem=out_recv_sem,
                device_id=(other, work),
                device_id_type=MESH,
            ).start()

    pltpu.make_async_copy(landed, landed, out_recv_sem).wait()
    for half in range(2):
        side(half).wait_send()
    pltpu.make_async_copy(send, send, send_sem).wait()

    @pl.when(adj & jnp.logical_not(itself))
    def _():
        sent = send.at[:, 0]
        pltpu.make_async_copy(sent, sent, adj_sem).wait()

    @pl.when(itself)
    def _():
        sent = send.at[pl.ds(0, 63), 0]
        pltpu.make_async_copy(sent, sent, adj_sem).wait()

    pltpu.make_async_copy(out_send, out_send, out_send_sem).wait()


def order_rows(landed, pre, grad, landed_v, out_v, landed_f, rows_f, in_sem, out_sem):
    loads = [pltpu.make_async_copy(landed.at[c], landed_v.at[c], in_sem.at[c]) for c in range(2)]
    stores = [pltpu.make_async_copy(out_v.at[c], out, out_sem.at[c]) for c, out in enumerate((pre, grad))]
    for load in loads:
        load.start()
    for c in range(2):
        loads[c].wait()
        landed_f[c] = landed_v[c].reshape(BLOCKS * 8, LANES).astype(jnp.float32)
        for ch in range(2):
            for p in range(2):
                for height in range(2):
                    rows_f[c, ch, p, pl.ds(height, BLOCKS, stride=2), :] = landed_f[
                        c, pl.ds(4 * p + 2 * height + ch, BLOCKS, stride=8), :
                    ]
                out_v[c, ch, p] = rows_f[c, ch, p].astype(jnp.bfloat16)
        stores[c].start()
    for store in stores:
        store.wait()


def body(activations, cotangent, relu_mask, weights):
    bf16, f32 = jnp.bfloat16, jnp.float32
    anywhere = pl.BlockSpec(memory_space=pl.ANY)
    dma = pltpu.SemaphoreType.DMA
    landed = pl.pallas_call(
        kernel,
        out_shape=jax.ShapeDtypeStruct((2, BLOCKS, 8, LANES), bf16),
        in_specs=[anywhere] * 4,
        out_specs=anywhere,
        scratch_shapes=[
            pltpu.VMEM((2, 2, 64, LANES), bf16),
            pltpu.VMEM((2, 2, 64, LANES), bf16),
            pltpu.VMEM((2, 2, 64, LANES), jnp.int32),
            pltpu.VMEM((3, 3, 3, LANES, LANES), bf16),
            pltpu.VMEM((2, 2, 2, 80, LANES), f32),
            pltpu.VMEM((2 * BLOCKS, 2, 8, LANES), bf16),
            pltpu.VMEM((2, 4, 32, 8, LANES), bf16),
            pltpu.VMEM((3, 2, 2, 3 * LANES, 2 * LANES), bf16),
            pltpu.VMEM((2, 3 * LANES, 2 * LANES), f32),
            pltpu.VMEM((2, 2, LANES, LANES), f32),
            pltpu.VMEM((64 * 8, LANES), f32),
            pltpu.VMEM((64, 8, LANES), bf16),
            dma((3,)),
            dma,
            dma,
            dma,
            dma((2,)),
            dma((2,)),
            dma((2,)),
            dma((2,)),
            dma,
            dma,
        ],
        compiler_params=pltpu.CompilerParams(
            collective_id=0, has_side_effects=True, vmem_limit_bytes=63 * 1024 * 1024
        ),
    )(activations, cotangent, relu_mask, weights)
    out = jax.ShapeDtypeStruct((2, 2, 64, LANES), bf16)
    return pl.pallas_call(
        order_rows,
        out_shape=(out, out),
        in_specs=[anywhere],
        out_specs=(anywhere, anywhere),
        scratch_shapes=[
            pltpu.VMEM((2, BLOCKS, 8, LANES), bf16),
            pltpu.VMEM((2, 2, 2, 64, LANES), bf16),
            pltpu.VMEM((2, BLOCKS * 8, LANES), f32),
            pltpu.VMEM((2, 2, 2, 64, LANES), f32),
            dma((2,)),
            dma((2,)),
        ],
        compiler_params=pltpu.CompilerParams(vmem_limit_bytes=63 * 1024 * 1024),
    )(landed)


def solution(mesh):
    placed = (
        P("chan", "slab", None, None),
        P("chan", "slab", None, None),
        P("chan", "slab", None, None),
        P(),
    )
    return jax.shard_map(
        body,
        mesh=mesh,
        in_specs=placed,
        out_specs=(P("chan", "slab", None, None), P("chan", "slab", None, None)),
        check_vma=False,
    )
```

```python
import jax
import jax.numpy as jnp
from jax import lax
from jax.experimental import pallas as pl
from jax.experimental.pallas import tpu as pltpu
from jax.sharding import PartitionSpec as P

MESH = pl.DeviceIdType.MESH
BLOCKS = 32
LANES = 128


def spread(height):
    ch = lax.broadcasted_iota(jnp.int32, (3 * LANES, 1), 0)
    tap, ch = lax.shift_right_logical(ch, 7), lax.bitwise_and(ch, 127)
    at = lax.broadcasted_iota(jnp.int32, (1, 4 * LANES), 1)
    z_hi = lax.shift_right_logical(at, 8)
    source = lax.bitwise_and(lax.shift_right_logical(at, 3), 31)
    chan = lax.shift_right_logical(source, 3) * 16 + z_hi * 8 + lax.bitwise_and(source, 7)
    channel = 2 * chan + lax.bitwise_and(lax.shift_right_logical(at, 2), 1)
    hit = (ch == channel) & (lax.bitwise_and(at, 3) == tap + height)
    return jnp.where(hit, 1.0, 0.0).astype(jnp.bfloat16)


def kernel(act, cot, mask, weights, landed, act_v, cot_v, mask_v, w_v, padded, send, recv, taps, part_f, rows_f, units_f,
           out_send, in_sem, w_sem, send_sem, adj_sem, recv_sem, adj_recv_sem, side_send_sem, side_recv_sem, out_send_sem,
           out_recv_sem):
    chan, slab = lax.axis_index("chan"), lax.axis_index("slab")
    z_hi = (chan // 8) % 2
    core = chan % 2
    beside = chan + 1 - 2 * core
    source = (chan // 16) * 8 + chan % 8
    pair = slab // 2
    adj = (slab == 1) | (slab == 2)
    my_block = ((chan // 16) * 4 + (chan // 2) % 4) * 2 + slab % 2
    work = 2 * (1 - slab // 2) + core
    work_inner = (work == 1) | (work == 2)
    work_adj = 3 - work
    itself = adj & (core == slab - 1)

    loads = [
        pltpu.make_async_copy(act, act_v, in_sem.at[0]),
        pltpu.make_async_copy(cot, cot_v, in_sem.at[1]),
        pltpu.make_async_copy(mask, mask_v, in_sem.at[2]),
    ]
    w_load = pltpu.make_async_copy(weights, w_v, w_sem)
    barrier = pltpu.get_barrier_semaphore()

    def greet(others, at_slab):
        for other in others:
            pl.semaphore_signal(barrier, inc=1, device_id=(other, at_slab), device_id_type=MESH)

    for part in range(8):
        others = range(8 * part, 8 * part + 8)
        greet(others, work)

        @pl.when(work_inner & ((work_adj != slab) | (chan // 8 != part)))
        def _():
            greet(others, work_adj)

        @pl.when(work_inner & (work_adj == slab) & (chan // 8 == part))
        def _():
            for other in others:

                @pl.when(other != chan)
                def _():
                    greet((other,), work_adj)

    greet((beside,), slab)

    for load in (*loads, w_load):
        load.start()

    for load in loads:
        load.wait()
    for c in range(2):
        for ch in range(2):
            for p in range(2):
                padded[c, ch, p, 0:8, :] = jnp.zeros((8, LANES), jnp.float32)
                padded[c, ch, p, 72:80, :] = jnp.zeros((8, LANES), jnp.float32)
    for ch in range(2):
        for p in range(2):
            padded[0, ch, p, 8:72, :] = act_v[ch, p].astype(jnp.float32)
            padded[1, ch, p, 8:72, :] = jnp.where(mask_v[ch, p] == 1, cot_v[ch, p].astype(jnp.float32), 0.0)
    for b in range(BLOCKS):
        for c in range(2):
            for p in range(2):
                window = [padded[c, ch, p, 7 + 2 * b : 11 + 2 * b, :] for ch in range(2)]
                send[2 * b + c, p] = jnp.concatenate(window, axis=0).astype(jnp.bfloat16)

    def make_taps(transposed):
        w_load.wait()
        for height in range(2):
            places = spread(height)
            for i in range(3):

                @pl.loop(0, 3)
                def _(k):
                    if transposed:
                        left = jnp.concatenate([w_v[2 - i, 2 - j, 2 - k] for j in range(3)], axis=0)
                        total = lax.dot_general(
                            left, places, (((0,), (0,)), ((), ())), preferred_element_type=jnp.float32
                        )
                    else:
                        left = jnp.concatenate([w_v[i, j, k] for j in range(3)], axis=1)
                        total = jnp.dot(left, places, preferred_element_type=jnp.float32)
                    at = pl.ds(pl.multiple_of(k * LANES, LANES), LANES)
                    for half in range(2):
                        taps[i, height, half, at, :] = total[:, 256 * half : 256 * (half + 1)].astype(jnp.bfloat16)

    @pl.when(z_hi == 0)
    def _():
        make_taps(False)

    pl.semaphore_wait(barrier, 65 + 64 * adj.astype(jnp.int32) - itself.astype(jnp.int32))

    for c in (1, 0):
        for b in range(BLOCKS):
            pltpu.make_async_remote_copy(
                src_ref=send.at[2 * b + c],
                dst_ref=recv.at[z_hi, pl.ds(1, 2), source],
                send_sem=send_sem,
                recv_sem=recv_sem.at[z_hi],
                device_id=((b // 8) * 16 + 8 * c + (b // 2 % 4) * 2 + slab % 2, 2 * (1 - pair) + b % 2),
                device_id_type=MESH,
            ).start()

    @pl.when(adj)
    def _():
        plane = 2 - slab
        there = 3 * (slab - 1)
        for c in (1, 0):
            for b in range(BLOCKS):
                other, at_slab = (b // 8) * 16 + 8 * c + (b // 2 % 4) * 2 + slab - 1, 2 * pair + b % 2

                @pl.when((other != chan) | (at_slab != slab))
                def _():
                    pltpu.make_async_remote_copy(
                        src_ref=send.at[2 * b + c, plane],
                        dst_ref=recv.at[z_hi, there, source],
                        send_sem=adj_sem,
                        recv_sem=adj_recv_sem.at[z_hi],
                        device_id=(other, at_slab),
                        device_id_type=MESH,
                    ).start()

        @pl.when(itself)
        def _():
            mine = send.at[2 * my_block + z_hi, plane]
            pltpu.make_async_copy(mine, recv.at[z_hi, there, source], adj_recv_sem.at[z_hi]).start()

    @pl.when(jnp.logical_not(work_inner))
    def _():
        recv[:, work] = jnp.zeros((2, 32, 8, LANES), jnp.bfloat16)

    @pl.when(z_hi == 1)
    def _():
        make_taps(True)

    def side(half):
        return pltpu.make_async_remote_copy(
            src_ref=recv.at[half, 2 - core],
            dst_ref=recv.at[half, 3 * core],
            send_sem=side_send_sem.at[half],
            recv_sem=side_recv_sem.at[half],
            device_id=(beside, slab),
            device_id_type=MESH,
        )

    def product(i, half, height):
        right = jnp.concatenate([recv[half, i + p].reshape(256, LANES) for p in range(2)], axis=1)
        return jnp.dot(taps[i, height, half], right, preferred_element_type=jnp.float32)

    last = 2 - 2 * core
    for turn in range(2):
        half = z_hi if turn == 0 else 1 - z_hi
        here = recv.at[half, pl.ds(1, 2)]
        pltpu.make_async_copy(here, here, recv_sem.at[half]).wait()
        side(half).start()
        for height in range(2):
            if turn == 0:
                part_f[height] = product(1, half, height)
            else:
                part_f[height] += product(1, half, height)

        @pl.when(work_inner)
        def _():
            here = recv.at[half, 3 * core]
            pltpu.make_async_copy(here, here, adj_recv_sem.at[half]).wait()

        for height in range(2):
            part_f[height] += product(2 - last, half, height)
        side(half).wait_recv()
        if turn == 0:
            for height in range(2):
                part_f[height] += product(last, half, height)

    col = lax.broadcasted_iota(jnp.int32, (LANES, LANES), 1)
    for height in range(2):
        part = part_f[height] + product(last, 1 - z_hi, height)
        for p in range(2):
            lanes = slice(LANES * p, LANES * (p + 1))
            before, here, after = (part[LANES * k : LANES * (k + 1), lanes] for k in range(3))
            rows_f[p, height] = (
                here
                + jnp.where(col == 0, 0.0, pltpu.roll(before, 1, 1))
                + jnp.where(col == LANES - 1, 0.0, pltpu.roll(after, LANES - 1, 1))
            )
    for p in range(2):
        for height in range(2):
            for ch in range(2):
                units_f[pl.ds(4 * p + 2 * height + ch, 64, stride=8), :] = rows_f[p, height, pl.ds(ch, 64, stride=2), :]
    out_send[...] = units_f[...].astype(jnp.bfloat16).reshape(64, 8, LANES)

    def gate(half):
        part = out_send.at[pl.ds(0, 32)]
        pltpu.make_async_copy(part, part, out_send_sem.at[half]).wait()

    for half in range(2):
        if half:
            gate(0)
        for step in range(32):
            other = (step // 8) * 16 + half * 8 + step % 8
            pltpu.make_async_remote_copy(
                src_ref=out_send.at[other],
                dst_ref=landed.at[z_hi, my_block],
                send_sem=out_send_sem.at[half],
                recv_sem=out_recv_sem,
                device_id=(other, work),
                device_id_type=MESH,
            ).start()

    pltpu.make_async_copy(landed, landed, out_recv_sem).wait()
    gate(1)
    for half in range(2):
        side(half).wait_send()
    pltpu.make_async_copy(send, send, send_sem).wait()

    @pl.when(adj & jnp.logical_not(itself))
    def _():
        sent = send.at[:, 0]
        pltpu.make_async_copy(sent, sent, adj_sem).wait()

    @pl.when(itself)
    def _():
        sent = send.at[pl.ds(0, 63), 0]
        pltpu.make_async_copy(sent, sent, adj_sem).wait()


def order_rows(landed, pre, grad, landed_v, out_v, landed_f, rows_f, in_sem, out_sem):
    loads = [pltpu.make_async_copy(landed.at[c], landed_v.at[c], in_sem.at[c]) for c in range(2)]
    stores = [pltpu.make_async_copy(out_v.at[c], out, out_sem.at[c]) for c, out in enumerate((pre, grad))]
    for load in loads:
        load.start()
    for c in range(2):
        loads[c].wait()
        landed_f[c] = landed_v[c].reshape(BLOCKS * 8, LANES).astype(jnp.float32)
        for ch in range(2):
            for p in range(2):
                for height in range(2):
                    rows_f[c, ch, p, pl.ds(height, BLOCKS, stride=2), :] = landed_f[
                        c, pl.ds(4 * p + 2 * height + ch, BLOCKS, stride=8), :
                    ]
                out_v[c, ch, p] = rows_f[c, ch, p].astype(jnp.bfloat16)
        stores[c].start()
    for store in stores:
        store.wait()


def body(activations, cotangent, relu_mask, weights):
    bf16, f32 = jnp.bfloat16, jnp.float32
    anywhere = pl.BlockSpec(memory_space=pl.ANY)
    dma = pltpu.SemaphoreType.DMA
    landed = pl.pallas_call(
        kernel,
        out_shape=jax.ShapeDtypeStruct((2, BLOCKS, 8, LANES), bf16),
        in_specs=[anywhere] * 4,
        out_specs=anywhere,
        scratch_shapes=[
            pltpu.VMEM((2, 2, 64, LANES), bf16),
            pltpu.VMEM((2, 2, 64, LANES), bf16),
            pltpu.VMEM((2, 2, 64, LANES), jnp.int32),
            pltpu.VMEM((3, 3, 3, LANES, LANES), bf16),
            pltpu.VMEM((2, 2, 2, 80, LANES), f32),
            pltpu.VMEM((2 * BLOCKS, 2, 8, LANES), bf16),
            pltpu.VMEM((2, 4, 32, 8, LANES), bf16),
            pltpu.VMEM((3, 2, 2, 3 * LANES, 2 * LANES), bf16),
            pltpu.VMEM((2, 3 * LANES, 2 * LANES), f32),
            pltpu.VMEM((2, 2, LANES, LANES), f32),
            pltpu.VMEM((64 * 8, LANES), f32),
            pltpu.VMEM((64, 8, LANES), bf16),
            dma((3,)),
            dma,
            dma,
            dma,
            dma((2,)),
            dma((2,)),
            dma((2,)),
            dma((2,)),
            dma((2,)),
            dma,
        ],
        compiler_params=pltpu.CompilerParams(
            collective_id=0, has_side_effects=True, vmem_limit_bytes=63 * 1024 * 1024
        ),
    )(activations, cotangent, relu_mask, weights)
    out = jax.ShapeDtypeStruct((2, 2, 64, LANES), bf16)
    return pl.pallas_call(
        order_rows,
        out_shape=(out, out),
        in_specs=[anywhere],
        out_specs=(anywhere, anywhere),
        scratch_shapes=[
            pltpu.VMEM((2, BLOCKS, 8, LANES), bf16),
            pltpu.VMEM((2, 2, 2, 64, LANES), bf16),
            pltpu.VMEM((2, BLOCKS * 8, LANES), f32),
            pltpu.VMEM((2, 2, 2, 64, LANES), f32),
            dma((2,)),
            dma((2,)),
        ],
        compiler_params=pltpu.CompilerParams(vmem_limit_bytes=63 * 1024 * 1024),
    )(landed)


def solution(mesh):
    placed = (
        P("chan", "slab", None, None),
        P("chan", "slab", None, None),
        P("chan", "slab", None, None),
        P(),
    )
    return jax.shard_map(
        body,
        mesh=mesh,
        in_specs=placed,
        out_specs=(P("chan", "slab", None, None), P("chan", "slab", None, None)),
        check_vma=False,
    )
```

```python
import jax
import jax.numpy as jnp
from jax import lax
from jax.experimental import pallas as pl
from jax.experimental.pallas import tpu as pltpu
from jax.sharding import PartitionSpec as P

MESH = pl.DeviceIdType.MESH
BLOCKS = 32
LANES = 128
FARTHEST_FIRST = sorted(
    ((dx, dy) for dx in range(4) for dy in range(4)),
    key=lambda d: (-min(d[0], 4 - d[0]) - min(d[1], 4 - d[1]), -min(d[0], 4 - d[0]), d),
)


def spread(height):
    ch = lax.broadcasted_iota(jnp.int32, (3 * LANES, 1), 0)
    tap, ch = lax.shift_right_logical(ch, 7), lax.bitwise_and(ch, 127)
    at = lax.broadcasted_iota(jnp.int32, (1, 4 * LANES), 1)
    z_hi = lax.shift_right_logical(at, 8)
    source = lax.bitwise_and(lax.shift_right_logical(at, 3), 31)
    chan = lax.shift_right_logical(source, 3) * 16 + z_hi * 8 + lax.bitwise_and(source, 7)
    channel = 2 * chan + lax.bitwise_and(lax.shift_right_logical(at, 2), 1)
    hit = (ch == channel) & (lax.bitwise_and(at, 3) == tap + height)
    return jnp.where(hit, 1.0, 0.0).astype(jnp.bfloat16)


def kernel(act, cot, mask, weights, landed, act_v, cot_v, mask_v, w_v, padded, send, recv, taps, part_f, rows_f, units_f,
           out_send, in_sem, w_sem, send_sem, adj_sem, recv_sem, adj_recv_sem, side_send_sem, side_recv_sem, out_send_sem,
           out_recv_sem):
    chan, slab = lax.axis_index("chan"), lax.axis_index("slab")
    z_hi = (chan // 8) % 2
    core = chan % 2
    beside = chan + 1 - 2 * core
    source = (chan // 16) * 8 + chan % 8
    pair = slab // 2
    adj = (slab == 1) | (slab == 2)
    my_block = ((chan // 16) * 4 + (chan // 2) % 4) * 2 + slab % 2
    work = 2 * (1 - slab // 2) + core
    work_inner = (work == 1) | (work == 2)
    work_adj = 3 - work
    spots = []
    for dx, dy in FARTHEST_FIRST:
        spots.append(((chan // 16 + dx) % 4, (chan // 2 % 4 + dy) % 4))
    itself = adj & (core == slab - 1)

    loads = [
        pltpu.make_async_copy(act, act_v, in_sem.at[0]),
        pltpu.make_async_copy(cot, cot_v, in_sem.at[1]),
        pltpu.make_async_copy(mask, mask_v, in_sem.at[2]),
    ]
    w_load = pltpu.make_async_copy(weights, w_v, w_sem)
    barrier = pltpu.get_barrier_semaphore()

    def greet(others, at_slab):
        for other in others:
            pl.semaphore_signal(barrier, inc=1, device_id=(other, at_slab), device_id_type=MESH)

    for part in range(8):
        others = range(8 * part, 8 * part + 8)
        greet(others, work)

        @pl.when(work_inner & ((work_adj != slab) | (chan // 8 != part)))
        def _():
            greet(others, work_adj)

        @pl.when(work_inner & (work_adj == slab) & (chan // 8 == part))
        def _():
            for other in others:

                @pl.when(other != chan)
                def _():
                    greet((other,), work_adj)

    greet((beside,), slab)

    for load in (*loads, w_load):
        load.start()

    for load in loads:
        load.wait()
    for c in range(2):
        for ch in range(2):
            for p in range(2):
                padded[c, ch, p, 0:8, :] = jnp.zeros((8, LANES), jnp.float32)
                padded[c, ch, p, 72:80, :] = jnp.zeros((8, LANES), jnp.float32)
    for ch in range(2):
        for p in range(2):
            padded[0, ch, p, 8:72, :] = act_v[ch, p].astype(jnp.float32)
            padded[1, ch, p, 8:72, :] = jnp.where(mask_v[ch, p] == 1, cot_v[ch, p].astype(jnp.float32), 0.0)
    for b in range(BLOCKS):
        for c in range(2):
            for p in range(2):
                window = [padded[c, ch, p, 7 + 2 * b : 11 + 2 * b, :] for ch in range(2)]
                send[2 * b + c, p] = jnp.concatenate(window, axis=0).astype(jnp.bfloat16)

    def make_taps(transposed):
        w_load.wait()
        for height in range(2):
            places = spread(height)
            for i in range(3):

                @pl.loop(0, 3)
                def _(k):
                    if transposed:
                        left = jnp.concatenate([w_v[2 - i, 2 - j, 2 - k] for j in range(3)], axis=0)
                        total = lax.dot_general(
                            left, places, (((0,), (0,)), ((), ())), preferred_element_type=jnp.float32
                        )
                    else:
                        left = jnp.concatenate([w_v[i, j, k] for j in range(3)], axis=1)
                        total = jnp.dot(left, places, preferred_element_type=jnp.float32)
                    at = pl.ds(pl.multiple_of(k * LANES, LANES), LANES)
                    for half in range(2):
                        taps[i, height, half, at, :] = total[:, 256 * half : 256 * (half + 1)].astype(jnp.bfloat16)

    @pl.when(z_hi == 0)
    def _():
        make_taps(False)

    pl.semaphore_wait(barrier, 65 + 64 * adj.astype(jnp.int32) - itself.astype(jnp.int32))

    for at_x, at_y, zb, c in [(*spot, zb, c) for spot in spots for c in (1, 0) for zb in range(2)]:
        pltpu.make_async_remote_copy(
            src_ref=send.at[16 * at_x + 4 * at_y + 2 * zb + c],
            dst_ref=recv.at[z_hi, pl.ds(1, 2), source],
            send_sem=send_sem,
            recv_sem=recv_sem.at[z_hi],
            device_id=(16 * at_x + 8 * c + 2 * at_y + slab % 2, 2 * (1 - pair) + zb),
            device_id_type=MESH,
        ).start()

    @pl.when(adj)
    def _():
        plane = 2 - slab
        there = 3 * (slab - 1)
        for at_x, at_y, zb, c in [(*spot, zb, c) for spot in spots for c in (1, 0) for zb in range(2)]:
            unit = 16 * at_x + 4 * at_y + 2 * zb + c
            other, at_slab = 16 * at_x + 8 * c + 2 * at_y + slab - 1, 2 * pair + zb

            @pl.when((other != chan) | (at_slab != slab))
            def _():
                pltpu.make_async_remote_copy(
                    src_ref=send.at[unit, plane],
                    dst_ref=recv.at[z_hi, there, source],
                    send_sem=adj_sem,
                    recv_sem=adj_recv_sem.at[z_hi],
                    device_id=(other, at_slab),
                    device_id_type=MESH,
                ).start()

        @pl.when(itself)
        def _():
            mine = send.at[2 * my_block + z_hi, plane]
            pltpu.make_async_copy(mine, recv.at[z_hi, there, source], adj_recv_sem.at[z_hi]).start()

    @pl.when(jnp.logical_not(work_inner))
    def _():
        recv[:, work] = jnp.zeros((2, 32, 8, LANES), jnp.bfloat16)

    @pl.when(z_hi == 1)
    def _():
        make_taps(True)

    def side(half):
        return pltpu.make_async_remote_copy(
            src_ref=recv.at[half, 2 - core],
            dst_ref=recv.at[half, 3 * core],
            send_sem=side_send_sem.at[half],
            recv_sem=side_recv_sem.at[half],
            device_id=(beside, slab),
            device_id_type=MESH,
        )

    def product(i, half, height):
        right = jnp.concatenate([recv[half, i + p].reshape(256, LANES) for p in range(2)], axis=1)
        return jnp.dot(taps[i, height, half], right, preferred_element_type=jnp.float32)

    last = 2 - 2 * core
    for turn in range(2):
        half = z_hi if turn == 0 else 1 - z_hi
        here = recv.at[half, pl.ds(1, 2)]
        pltpu.make_async_copy(here, here, recv_sem.at[half]).wait()
        side(half).start()
        for height in range(2):
            if turn == 0:
                part_f[height] = product(1, half, height)
            else:
                part_f[height] += product(1, half, height)

        @pl.when(work_inner)
        def _():
            here = recv.at[half, 3 * core]
            pltpu.make_async_copy(here, here, adj_recv_sem.at[half]).wait()

        for height in range(2):
            part_f[height] += product(2 - last, half, height)
        side(half).wait_recv()
        if turn == 0:
            for height in range(2):
                part_f[height] += product(last, half, height)

    col = lax.broadcasted_iota(jnp.int32, (LANES, LANES), 1)
    for height in range(2):
        part = part_f[height] + product(last, 1 - z_hi, height)
        for p in range(2):
            lanes = slice(LANES * p, LANES * (p + 1))
            before, here, after = (part[LANES * k : LANES * (k + 1), lanes] for k in range(3))
            rows_f[p, height] = (
                here
                + jnp.where(col == 0, 0.0, pltpu.roll(before, 1, 1))
                + jnp.where(col == LANES - 1, 0.0, pltpu.roll(after, LANES - 1, 1))
            )
    for p in range(2):
        for height in range(2):
            for ch in range(2):
                units_f[pl.ds(4 * p + 2 * height + ch, 64, stride=8), :] = rows_f[p, height, pl.ds(ch, 64, stride=2), :]
    out_send[...] = units_f[...].astype(jnp.bfloat16).reshape(64, 8, LANES)

    def gate(half):
        part = out_send.at[pl.ds(0, 32)]
        pltpu.make_async_copy(part, part, out_send_sem.at[half]).wait()

    for half in range(2):
        if half:
            gate(0)
        for step in range(32):
            other = (step // 8) * 16 + half * 8 + step % 8
            pltpu.make_async_remote_copy(
                src_ref=out_send.at[other],
                dst_ref=landed.at[z_hi, my_block],
                send_sem=out_send_sem.at[half],
                recv_sem=out_recv_sem,
                device_id=(other, work),
                device_id_type=MESH,
            ).start()

    pltpu.make_async_copy(landed, landed, out_recv_sem).wait()
    gate(1)
    for half in range(2):
        side(half).wait_send()
    pltpu.make_async_copy(send, send, send_sem).wait()

    @pl.when(adj & jnp.logical_not(itself))
    def _():
        sent = send.at[:, 0]
        pltpu.make_async_copy(sent, sent, adj_sem).wait()

    @pl.when(itself)
    def _():
        sent = send.at[pl.ds(0, 63), 0]
        pltpu.make_async_copy(sent, sent, adj_sem).wait()


def order_rows(landed, pre, grad, landed_v, out_v, landed_f, rows_f, in_sem, out_sem):
    loads = [pltpu.make_async_copy(landed.at[c], landed_v.at[c], in_sem.at[c]) for c in range(2)]
    stores = [pltpu.make_async_copy(out_v.at[c], out, out_sem.at[c]) for c, out in enumerate((pre, grad))]
    for load in loads:
        load.start()
    for c in range(2):
        loads[c].wait()
        landed_f[c] = landed_v[c].reshape(BLOCKS * 8, LANES).astype(jnp.float32)
        for ch in range(2):
            for p in range(2):
                for height in range(2):
                    rows_f[c, ch, p, pl.ds(height, BLOCKS, stride=2), :] = landed_f[
                        c, pl.ds(4 * p + 2 * height + ch, BLOCKS, stride=8), :
                    ]
                out_v[c, ch, p] = rows_f[c, ch, p].astype(jnp.bfloat16)
        stores[c].start()
    for store in stores:
        store.wait()


def body(activations, cotangent, relu_mask, weights):
    bf16, f32 = jnp.bfloat16, jnp.float32
    anywhere = pl.BlockSpec(memory_space=pl.ANY)
    dma = pltpu.SemaphoreType.DMA
    landed = pl.pallas_call(
        kernel,
        out_shape=jax.ShapeDtypeStruct((2, BLOCKS, 8, LANES), bf16),
        in_specs=[anywhere] * 4,
        out_specs=anywhere,
        scratch_shapes=[
            pltpu.VMEM((2, 2, 64, LANES), bf16),
            pltpu.VMEM((2, 2, 64, LANES), bf16),
            pltpu.VMEM((2, 2, 64, LANES), jnp.int32),
            pltpu.VMEM((3, 3, 3, LANES, LANES), bf16),
            pltpu.VMEM((2, 2, 2, 80, LANES), f32),
            pltpu.VMEM((2 * BLOCKS, 2, 8, LANES), bf16),
            pltpu.VMEM((2, 4, 32, 8, LANES), bf16),
            pltpu.VMEM((3, 2, 2, 3 * LANES, 2 * LANES), bf16),
            pltpu.VMEM((2, 3 * LANES, 2 * LANES), f32),
            pltpu.VMEM((2, 2, LANES, LANES), f32),
            pltpu.VMEM((64 * 8, LANES), f32),
            pltpu.VMEM((64, 8, LANES), bf16),
            dma((3,)),
            dma,
            dma,
            dma,
            dma((2,)),
            dma((2,)),
            dma((2,)),
            dma((2,)),
            dma((2,)),
            dma,
        ],
        compiler_params=pltpu.CompilerParams(
            collective_id=0, has_side_effects=True, vmem_limit_bytes=63 * 1024 * 1024
        ),
    )(activations, cotangent, relu_mask, weights)
    out = jax.ShapeDtypeStruct((2, 2, 64, LANES), bf16)
    return pl.pallas_call(
        order_rows,
        out_shape=(out, out),
        in_specs=[anywhere],
        out_specs=(anywhere, anywhere),
        scratch_shapes=[
            pltpu.VMEM((2, BLOCKS, 8, LANES), bf16),
            pltpu.VMEM((2, 2, 2, 64, LANES), bf16),
            pltpu.VMEM((2, BLOCKS * 8, LANES), f32),
            pltpu.VMEM((2, 2, 2, 64, LANES), f32),
            dma((2,)),
            dma((2,)),
        ],
        compiler_params=pltpu.CompilerParams(vmem_limit_bytes=63 * 1024 * 1024),
    )(landed)


def solution(mesh):
    placed = (
        P("chan", "slab", None, None),
        P("chan", "slab", None, None),
        P("chan", "slab", None, None),
        P(),
    )
    return jax.shard_map(
        body,
        mesh=mesh,
        in_specs=placed,
        out_specs=(P("chan", "slab", None, None), P("chan", "slab", None, None)),
        check_vma=False,
    )
```

```python
import jax
import jax.numpy as jnp
from jax import lax
from jax.experimental import pallas as pl
from jax.experimental.pallas import tpu as pltpu
from jax.sharding import PartitionSpec as P

MESH = pl.DeviceIdType.MESH
BLOCKS = 32
LANES = 128
FARTHEST_FIRST = sorted(
    ((dx, dy) for dx in range(4) for dy in range(4)),
    key=lambda d: (-min(d[0], 4 - d[0]) - min(d[1], 4 - d[1]), -min(d[0], 4 - d[0]), d),
)


def spread(height):
    ch = lax.broadcasted_iota(jnp.int32, (3 * LANES, 1), 0)
    tap, ch = lax.shift_right_logical(ch, 7), lax.bitwise_and(ch, 127)
    at = lax.broadcasted_iota(jnp.int32, (1, 4 * LANES), 1)
    z_hi = lax.shift_right_logical(at, 8)
    source = lax.bitwise_and(lax.shift_right_logical(at, 3), 31)
    chan = lax.shift_right_logical(source, 3) * 16 + z_hi * 8 + lax.bitwise_and(source, 7)
    channel = 2 * chan + lax.bitwise_and(lax.shift_right_logical(at, 2), 1)
    hit = (ch == channel) & (lax.bitwise_and(at, 3) == tap + height)
    return jnp.where(hit, 1.0, 0.0).astype(jnp.bfloat16)


def kernel(act, cot, mask, weights, landed, act_v, cot_v, mask_v, w_v, padded, send, recv, taps, part_f, rows_f, units_f,
           out_send, in_sem, w_sem, send_sem, adj_sem, recv_sem, adj_recv_sem, side_send_sem, side_recv_sem, out_send_sem,
           out_recv_sem):
    chan, slab = lax.axis_index("chan"), lax.axis_index("slab")
    z_hi = (chan // 8) % 2
    core = chan % 2
    beside = chan + 1 - 2 * core
    source = (chan // 16) * 8 + chan % 8
    pair = slab // 2
    adj = (slab == 1) | (slab == 2)
    my_block = ((chan // 16) * 4 + (chan // 2) % 4) * 2 + slab % 2
    work = 2 * (1 - slab // 2) + core
    work_inner = (work == 1) | (work == 2)
    work_adj = 3 - work
    spots = []
    for dx, dy in FARTHEST_FIRST:
        spots.append(((chan // 16 + dx) % 4, (chan // 2 % 4 + dy) % 4))
    itself = adj & (core == slab - 1)

    loads = [
        pltpu.make_async_copy(act, act_v, in_sem.at[0]),
        pltpu.make_async_copy(cot, cot_v, in_sem.at[1]),
        pltpu.make_async_copy(mask, mask_v, in_sem.at[2]),
    ]
    w_load = pltpu.make_async_copy(weights, w_v, w_sem)
    barrier = pltpu.get_barrier_semaphore()

    def greet(others, at_slab):
        for other in others:
            pl.semaphore_signal(barrier, inc=1, device_id=(other, at_slab), device_id_type=MESH)

    for part in range(8):
        others = range(8 * part, 8 * part + 8)
        greet(others, work)

        @pl.when(work_inner & ((work_adj != slab) | (chan // 8 != part)))
        def _():
            greet(others, work_adj)

        @pl.when(work_inner & (work_adj == slab) & (chan // 8 == part))
        def _():
            for other in others:

                @pl.when(other != chan)
                def _():
                    greet((other,), work_adj)

    greet((beside,), slab)

    for load in (*loads, w_load):
        load.start()

    for load in loads:
        load.wait()
    for c in range(2):
        for ch in range(2):
            for p in range(2):
                padded[c, ch, p, 0:8, :] = jnp.zeros((8, LANES), jnp.float32)
                padded[c, ch, p, 72:80, :] = jnp.zeros((8, LANES), jnp.float32)
    for ch in range(2):
        for p in range(2):
            padded[0, ch, p, 8:72, :] = act_v[ch, p].astype(jnp.float32)
            padded[1, ch, p, 8:72, :] = jnp.where(mask_v[ch, p] == 1, cot_v[ch, p].astype(jnp.float32), 0.0)
    for b in range(BLOCKS):
        for c in range(2):
            for p in range(2):
                window = [padded[c, ch, p, 7 + 2 * b : 11 + 2 * b, :] for ch in range(2)]
                send[2 * b + c, p] = jnp.concatenate(window, axis=0).astype(jnp.bfloat16)

    def make_taps(transposed):
        w_load.wait()
        for height in range(2):
            places = spread(height)
            for i in range(3):

                @pl.loop(0, 3)
                def _(k):
                    if transposed:
                        left = jnp.concatenate([w_v[2 - i, 2 - j, 2 - k] for j in range(3)], axis=0)
                        total = lax.dot_general(
                            left, places, (((0,), (0,)), ((), ())), preferred_element_type=jnp.float32
                        )
                    else:
                        left = jnp.concatenate([w_v[i, j, k] for j in range(3)], axis=1)
                        total = jnp.dot(left, places, preferred_element_type=jnp.float32)
                    at = pl.ds(pl.multiple_of(k * LANES, LANES), LANES)
                    for half in range(2):
                        taps[i, height, half, at, :] = total[:, 256 * half : 256 * (half + 1)].astype(jnp.bfloat16)

    @pl.when(z_hi == 0)
    def _():
        make_taps(False)

    pl.semaphore_wait(barrier, 65 + 64 * adj.astype(jnp.int32) - itself.astype(jnp.int32))

    for at_x, at_y, zb, c in [(*spot, zb, c) for spot in spots for c in (1, 0) for zb in range(2)]:
        pltpu.make_async_remote_copy(
            src_ref=send.at[16 * at_x + 4 * at_y + 2 * zb + c],
            dst_ref=recv.at[z_hi, pl.ds(1, 2), source],
            send_sem=send_sem,
            recv_sem=recv_sem.at[z_hi],
            device_id=(16 * at_x + 8 * c + 2 * at_y + slab % 2, 2 * (1 - pair) + zb),
            device_id_type=MESH,
        ).start()

    @pl.when(adj)
    def _():
        plane = 2 - slab
        there = 3 * (slab - 1)
        for at_x, at_y, zb, c in [(*spot, zb, c) for spot in spots for c in (1, 0) for zb in range(2)]:
            unit = 16 * at_x + 4 * at_y + 2 * zb + c
            other, at_slab = 16 * at_x + 8 * c + 2 * at_y + slab - 1, 2 * pair + zb

            @pl.when((other != chan) | (at_slab != slab))
            def _():
                pltpu.make_async_remote_copy(
                    src_ref=send.at[unit, plane],
                    dst_ref=recv.at[z_hi, there, source],
                    send_sem=adj_sem,
                    recv_sem=adj_recv_sem.at[z_hi],
                    device_id=(other, at_slab),
                    device_id_type=MESH,
                ).start()

        @pl.when(itself)
        def _():
            mine = send.at[2 * my_block + z_hi, plane]
            pltpu.make_async_copy(mine, recv.at[z_hi, there, source], adj_recv_sem.at[z_hi]).start()

    @pl.when(jnp.logical_not(work_inner))
    def _():
        recv[:, work] = jnp.zeros((2, 32, 8, LANES), jnp.bfloat16)

    @pl.when(z_hi == 1)
    def _():
        make_taps(True)

    def side(half):
        return pltpu.make_async_remote_copy(
            src_ref=recv.at[half, 2 - core],
            dst_ref=recv.at[half, 3 * core],
            send_sem=side_send_sem.at[half],
            recv_sem=side_recv_sem.at[half],
            device_id=(beside, slab),
            device_id_type=MESH,
        )

    def product(i, half, height):
        right = jnp.concatenate([recv[half, i + p].reshape(256, LANES) for p in range(2)], axis=1)
        return jnp.dot(taps[i, height, half], right, preferred_element_type=jnp.float32)

    last = 2 - 2 * core
    for turn in range(2):
        half = z_hi if turn == 0 else 1 - z_hi
        here = recv.at[half, pl.ds(1, 2)]
        pltpu.make_async_copy(here, here, recv_sem.at[half]).wait()
        side(half).start()
        for height in range(2):
            if turn == 0:
                part_f[height] = product(1, half, height)
            else:
                part_f[height] += product(1, half, height)

        @pl.when(work_inner)
        def _():
            here = recv.at[half, 3 * core]
            pltpu.make_async_copy(here, here, adj_recv_sem.at[half]).wait()

        for height in range(2):
            part_f[height] += product(2 - last, half, height)
        side(half).wait_recv()
        if turn == 0:
            for height in range(2):
                part_f[height] += product(last, half, height)

    col = lax.broadcasted_iota(jnp.int32, (LANES, LANES), 1)
    for height in range(2):
        part = part_f[height] + product(last, 1 - z_hi, height)
        for p in range(2):
            lanes = slice(LANES * p, LANES * (p + 1))
            before, here, after = (part[LANES * k : LANES * (k + 1), lanes] for k in range(3))
            rows_f[p, height] = (
                here
                + jnp.where(col == 0, 0.0, pltpu.roll(before, 1, 1))
                + jnp.where(col == LANES - 1, 0.0, pltpu.roll(after, LANES - 1, 1))
            )
    for p in range(2):
        for height in range(2):
            for ch in range(2):
                units_f[pl.ds(4 * p + 2 * height + ch, 64, stride=8), :] = rows_f[p, height, pl.ds(ch, 64, stride=2), :]
    out_send[...] = units_f[...].astype(jnp.bfloat16).reshape(64, 8, LANES)

    def gate(half):
        part = out_send.at[pl.ds(0, 32)]
        pltpu.make_async_copy(part, part, out_send_sem.at[half]).wait()

    for half in range(2):
        if half:
            gate(0)
        for step in range(32):
            other = (step // 8) * 16 + half * 8 + (step % 8 + 1 - 2 * (step % 2))
            pltpu.make_async_remote_copy(
                src_ref=out_send.at[other],
                dst_ref=landed.at[z_hi, my_block],
                send_sem=out_send_sem.at[half],
                recv_sem=out_recv_sem,
                device_id=(other, work),
                device_id_type=MESH,
            ).start()

    pltpu.make_async_copy(landed, landed, out_recv_sem).wait()
    gate(1)
    for half in range(2):
        side(half).wait_send()
    pltpu.make_async_copy(send, send, send_sem).wait()

    @pl.when(adj & jnp.logical_not(itself))
    def _():
        sent = send.at[:, 0]
        pltpu.make_async_copy(sent, sent, adj_sem).wait()

    @pl.when(itself)
    def _():
        sent = send.at[pl.ds(0, 63), 0]
        pltpu.make_async_copy(sent, sent, adj_sem).wait()


def order_rows(landed, pre, grad, landed_v, out_v, landed_f, rows_f, in_sem, out_sem):
    loads = [pltpu.make_async_copy(landed.at[c], landed_v.at[c], in_sem.at[c]) for c in range(2)]
    stores = [pltpu.make_async_copy(out_v.at[c], out, out_sem.at[c]) for c, out in enumerate((pre, grad))]
    for load in loads:
        load.start()
    for c in range(2):
        loads[c].wait()
        landed_f[c] = landed_v[c].reshape(BLOCKS * 8, LANES).astype(jnp.float32)
        for ch in range(2):
            for p in range(2):
                for height in range(2):
                    rows_f[c, ch, p, pl.ds(height, BLOCKS, stride=2), :] = landed_f[
                        c, pl.ds(4 * p + 2 * height + ch, BLOCKS, stride=8), :
                    ]
                out_v[c, ch, p] = rows_f[c, ch, p].astype(jnp.bfloat16)
        stores[c].start()
    for store in stores:
        store.wait()


def body(activations, cotangent, relu_mask, weights):
    bf16, f32 = jnp.bfloat16, jnp.float32
    anywhere = pl.BlockSpec(memory_space=pl.ANY)
    dma = pltpu.SemaphoreType.DMA
    landed = pl.pallas_call(
        kernel,
        out_shape=jax.ShapeDtypeStruct((2, BLOCKS, 8, LANES), bf16),
        in_specs=[anywhere] * 4,
        out_specs=anywhere,
        scratch_shapes=[
            pltpu.VMEM((2, 2, 64, LANES), bf16),
            pltpu.VMEM((2, 2, 64, LANES), bf16),
            pltpu.VMEM((2, 2, 64, LANES), jnp.int32),
            pltpu.VMEM((3, 3, 3, LANES, LANES), bf16),
            pltpu.VMEM((2, 2, 2, 80, LANES), f32),
            pltpu.VMEM((2 * BLOCKS, 2, 8, LANES), bf16),
            pltpu.VMEM((2, 4, 32, 8, LANES), bf16),
            pltpu.VMEM((3, 2, 2, 3 * LANES, 2 * LANES), bf16),
            pltpu.VMEM((2, 3 * LANES, 2 * LANES), f32),
            pltpu.VMEM((2, 2, LANES, LANES), f32),
            pltpu.VMEM((64 * 8, LANES), f32),
            pltpu.VMEM((64, 8, LANES), bf16),
            dma((3,)),
            dma,
            dma,
            dma,
            dma((2,)),
            dma((2,)),
            dma((2,)),
            dma((2,)),
            dma((2,)),
            dma,
        ],
        compiler_params=pltpu.CompilerParams(
            collective_id=0, has_side_effects=True, vmem_limit_bytes=63 * 1024 * 1024
        ),
    )(activations, cotangent, relu_mask, weights)
    out = jax.ShapeDtypeStruct((2, 2, 64, LANES), bf16)
    return pl.pallas_call(
        order_rows,
        out_shape=(out, out),
        in_specs=[anywhere],
        out_specs=(anywhere, anywhere),
        scratch_shapes=[
            pltpu.VMEM((2, BLOCKS, 8, LANES), bf16),
            pltpu.VMEM((2, 2, 2, 64, LANES), bf16),
            pltpu.VMEM((2, BLOCKS * 8, LANES), f32),
            pltpu.VMEM((2, 2, 2, 64, LANES), f32),
            dma((2,)),
            dma((2,)),
        ],
        compiler_params=pltpu.CompilerParams(vmem_limit_bytes=63 * 1024 * 1024),
    )(landed)


def solution(mesh):
    placed = (
        P("chan", "slab", None, None),
        P("chan", "slab", None, None),
        P("chan", "slab", None, None),
        P(),
    )
    return jax.shard_map(
        body,
        mesh=mesh,
        in_specs=placed,
        out_specs=(P("chan", "slab", None, None), P("chan", "slab", None, None)),
        check_vma=False,
    )
```
